32 devices in a mesh: dp: 16 (over z, y, core), tensor: 2 (over x).
Axes of the slice: x: 2, y: 2, z: 4, core: 2. Of those that a mesh axis runs over, the one named last changes fastest.
Arguments:
- projected: bfloat16 [3, 8192, 2560], P(None, 'dp', 'tensor'), may hold values from -40 to 40
- residue_counts: int32 [16], P('dp'), may hold values from 64 to 512, as said below
- migrate_plan: int32 [16], P('dp'), may hold values from 0 to 1, as said below
- out_weight: bfloat16 [2560, 2560], P('tensor', 'dp'), may hold values from -0.125 to 0.125
- out_cotangent: bfloat16 [32, 512, 2560], P('dp', None, 'tensor'), may hold values from -6 to 6
Outputs:
- layer_out: bfloat16 [32, 512, 2560], P('dp', None, 'tensor')
- grad_projected: bfloat16 [3, 8192, 2560], P(None, 'dp', 'tensor')
- grad_weight: float32 [2560, 2560], P('tensor', 'dp')
The draws below stay inside these ranges and needn't reach their ends.
Inputs may be any that keep to these rules, and one draw needn't show every extreme that they name: `residue_counts`: some tile has all 512 positions real, and some has exactly 64. migrate_plan[o] = 1 exactly where the sum of residue_counts over the 1 tiles of o exceeds that of its partner (o + 8) % 16 by more than 128, else 0; so never both devices of a pair have 1.
All inputs are finite; a program needn't handle non-finite values.
Results may differ from the reference program's by a relative error of at most 0.02.
Values may be sent and summed in bfloat16 or wider, within the bound.
A program may use at most 128 MiB of HBM per device.

```python
import jax
import jax.numpy as jnp
from jax import lax

D = 2560
HEAD_DIM = 64
TILE = 512
HOME = 1
TILES = 16
SLOTS = 32
TOKENS = 8192
N_DP = 16
N_TENSOR = 2


def draw_projected(key, part):
    key_base = jax.random.fold_in(key, 11)
    base = jax.random.normal(key_base, (3, TOKENS, D), jnp.float32)
    scaled = jnp.concatenate([base[0:2] * 2.0, base[2:3]], axis=0)
    result = jnp.clip(scaled, -12.0, 12.0)
    return result.astype(jnp.bfloat16)


def shared_counts(key):
    drawn = jax.random.randint(jax.random.fold_in(key, 21), (TILES,), TILE // 8, TILE + 1, jnp.int32)
    drawn = drawn.at[0].set(TILE)
    drawn = drawn.at[1].set(TILE // 8)
    return drawn.astype(jnp.int32)


def draw_residue_counts(key, part):
    return shared_counts(key)


def draw_migrate_plan(key, part):
    counts = shared_counts(key)
    device_load = jnp.sum(counts.reshape(N_DP, HOME), axis=1).astype(jnp.int32)
    partner_load = jnp.roll(device_load, -(N_DP // 2))
    return (device_load > partner_load + TILE // 4).astype(jnp.int32)


def steps_of(own_key, dims, split, smallest, largest):
    loudness = 1.0
    for dim, blocks in split:
        heights = jax.random.uniform(jax.random.fold_in(jax.random.fold_in(own_key, 6), dim), (blocks,), jnp.float32, smallest / len(split), largest / len(split))
        loudness = loudness * jnp.repeat(jnp.exp(heights), dims[dim] // blocks).reshape((-1,) + (1,) * (len(dims) - 1 - dim))
    return loudness


def bell_draw(key, extent, scale, bound, pieces=(), held_as=jnp.bfloat16):
    factor_of = steps_of(key, extent, pieces, -0.22, 0.18) if pieces else 1.0
    values = jax.random.normal(key, extent, jnp.float32) * scale * factor_of
    return jnp.minimum(jnp.maximum(values, -bound), bound).astype(held_as)


def setup_inputs(seed: int = 0) -> dict:
    seeds = jax.random.split(jax.random.key(seed), 6)
    projected = draw_projected(jax.random.fold_in(seeds[5], 71), 0)
    residue_counts = draw_residue_counts(jax.random.fold_in(seeds[5], 71), 0)
    migrate_plan = draw_migrate_plan(jax.random.fold_in(seeds[5], 71), 0)
    out_weight = bell_draw(seeds[3], (D, D), D ** -0.5, 0.125, ((0, 2), (1, 16)))
    out_cotangent = bell_draw(seeds[4], (SLOTS, TILE, D), 1.0, 6.0, ((0, 16), (2, 2)))
    return dict(projected=projected, residue_counts=residue_counts, migrate_plan=migrate_plan, out_weight=out_weight, out_cotangent=out_cotangent)


def attend(tile_qkv, count):
    length = tile_qkv.shape[1]
    columns = tile_qkv.shape[2]
    head_count = columns // HEAD_DIM
    queries = tile_qkv[0].astype(jnp.float32).reshape(length, head_count, HEAD_DIM)
    key_rows = tile_qkv[1].astype(jnp.float32).reshape(length, head_count, HEAD_DIM)
    values = tile_qkv[2].astype(jnp.float32).reshape(length, head_count, HEAD_DIM)
    scores = jnp.einsum('qhd,khd->hqk', queries, key_rows) * HEAD_DIM ** (-0.5)
    position = lax.iota(jnp.int32, length)
    live_mask = position < count
    scores = jnp.where(live_mask[None, None, :], scores, -1000000000.0)
    row_max = lax.optimization_barrier(jnp.max(scores, axis=2, keepdims=True))
    exponent = jnp.exp(scores - row_max)
    weights = (exponent / lax.optimization_barrier(jnp.sum(exponent, axis=2, keepdims=True))).astype(jnp.bfloat16)
    context = jnp.einsum('hqk,khd->qhd', weights.astype(jnp.float32), values)
    context = context * live_mask.astype(jnp.float32)[:, None, None]
    return context.reshape(length, columns)

def reference(projected, residue_counts, migrate_plan, out_weight, out_cotangent):
    tiles_all = N_DP * HOME
    slots_all = N_DP * (HOME + 1)
    group_width = D // N_TENSOR
    home_qkv = jnp.transpose(projected.reshape(3, tiles_all, TILE, D), (1, 0, 2, 3))
    context = lax.map(lambda packed: attend(packed[0], packed[1]).astype(jnp.bfloat16), (home_qkv, residue_counts))
    owner_dev = lax.iota(jnp.int32, tiles_all) // HOME
    home_place = lax.iota(jnp.int32, tiles_all) % HOME
    migrated = (home_place == HOME - 1) & (migrate_plan[owner_dev] == 1)
    helper = (owner_dev + N_DP // 2) % N_DP
    slot_index = jnp.where(migrated, helper * (HOME + 1) + HOME, owner_dev * (HOME + 1) + home_place).astype(jnp.int32)
    placed = jnp.zeros((slots_all, TILE, D), jnp.bfloat16).at[slot_index].set(context)
    flat_ctx = placed.reshape(slots_all * TILE, D)
    running = jnp.zeros((slots_all * TILE, D), jnp.float32)
    for block_index in range(N_TENSOR):
        lower = block_index * group_width
        partial_value = jnp.dot(flat_ctx[:, lower:lower + group_width], out_weight[lower:lower + group_width], preferred_element_type=jnp.float32)
        partial_value = lax.optimization_barrier(partial_value.astype(jnp.bfloat16)).astype(jnp.float32)
        running = running + partial_value
    layer_out = running.astype(jnp.bfloat16).reshape(slots_all, TILE, D)
    flat_cot = out_cotangent.reshape(slots_all * TILE, D)
    grad_context = jnp.dot(flat_cot, out_weight.T, preferred_element_type=jnp.float32).astype(jnp.bfloat16)
    grad_context = grad_context.reshape(slots_all, TILE, D)
    grad_weight = jnp.dot(flat_ctx.T, flat_cot, preferred_element_type=jnp.float32)
    cotangent = grad_context[slot_index]

    def tile_back(packed):
        tile_qkv, count, tile_cot = packed
        _, pullback = jax.vjp(lambda operand: attend(operand, count), tile_qkv)
        return pullback(tile_cot.astype(jnp.float32))[0]
    slot_grads = lax.map(tile_back, (home_qkv, residue_counts, cotangent))
    grad_projected = jnp.transpose(slot_grads, (1, 0, 2, 3)).reshape(3, tiles_all * TILE, D).astype(jnp.bfloat16)
    return (layer_out, grad_projected, grad_weight)
```

```python
import functools

import jax
import jax.numpy as jnp
from jax import lax
from jax.experimental import pallas as pl
from jax.experimental.pallas import tpu as pltpu
from jax.sharding import PartitionSpec as P

HEAD_DIM = 64
SCALE = HEAD_DIM ** (-0.5)
LOG2E = 1.4426950408889634
NT = (((1,), (1,)), ((), ()))
NN = (((1,), (0,)), ((), ()))
TN = (((0,), (0,)), ((), ()))


def dot(a, b, dims):
    return lax.dot_general(a, b, dims, preferred_element_type=jnp.float32)


def probs_t(k, q, live_keys):
    s = dot(k, q, NT) * (SCALE * LOG2E)
    s = jnp.where(live_keys, s, -1000000000.0)
    e = jnp.exp2(s - jnp.max(s, axis=0, keepdims=True))
    return e * (1.0 / jnp.sum(e, axis=0, keepdims=True))


def fwd_kernel(count_ref, qkv_ref, ctx_ref):
    length, width = ctx_ref.shape
    live = lax.broadcasted_iota(jnp.int32, (length, 1), 0) < count_ref[0]
    parts = []
    for h in range(width // HEAD_DIM):
        cols = slice(h * HEAD_DIM, (h + 1) * HEAD_DIM)
        p = probs_t(qkv_ref[1, :, cols], qkv_ref[0, :, cols], live).astype(jnp.bfloat16)
        parts.append(dot(p, qkv_ref[2, :, cols], TN))
    ctx = jnp.concatenate(parts, axis=1)
    ctx_ref[...] = jnp.where(live, ctx, 0.0).astype(jnp.bfloat16)


def bwd_kernel(count_ref, qkv_ref, cot_ref, out_ref):
    length, width = cot_ref.shape
    live = lax.broadcasted_iota(jnp.int32, (length, 1), 0) < count_ref[0]
    grads = ([], [], [])
    for h in range(width // HEAD_DIM):
        cols = slice(h * HEAD_DIM, (h + 1) * HEAD_DIM)
        q, k, v = qkv_ref[0, :, cols], qkv_ref[1, :, cols], qkv_ref[2, :, cols]
        cot = jnp.where(live, cot_ref[:, cols], jnp.bfloat16(0))
        p = probs_t(k, q, live)
        dp = dot(v, cot, NT).astype(jnp.bfloat16).astype(jnp.float32)
        t = p * dp
        ds = (t - p * jnp.sum(t, axis=0, keepdims=True)).astype(jnp.bfloat16)
        grads[0].append(dot(ds, k, TN) * SCALE)
        grads[1].append(dot(ds, q, NN) * SCALE)
        grads[2].append(dot(p.astype(jnp.bfloat16), cot, NN))
    for i in range(3):
        out_ref[i] = jnp.concatenate(grads[i], axis=1).astype(jnp.bfloat16)


def block_width(columns):
    return 128 if columns % 128 == 0 else columns


def attend(qkv, count):
    _, length, columns = qkv.shape
    bw = block_width(columns)
    return pl.pallas_call(
        fwd_kernel,
        grid=(columns // bw,),
        in_specs=[
            pl.BlockSpec(memory_space=pltpu.SMEM),
            pl.BlockSpec((3, length, bw), lambda i: (0, 0, i)),
        ],
        out_specs=pl.BlockSpec((length, bw), lambda i: (0, i)),
        out_shape=jax.ShapeDtypeStruct((length, columns), jnp.bfloat16),
        compiler_params=pltpu.CompilerParams(vmem_limit_bytes=32 << 20),
        cost_estimate=pl.CostEstimate(
            flops=20 * length * length * columns, bytes_accessed=8 * length * columns, transcendentals=0
        ),
        name="attend",
    )(count, qkv)


def attend_back(qkv, count, cot):
    _, length, columns = qkv.shape
    bw = block_width(columns)
    return pl.pallas_call(
        bwd_kernel,
        grid=(columns // bw,),
        in_specs=[
            pl.BlockSpec(memory_space=pltpu.SMEM),
            pl.BlockSpec((3, length, bw), lambda i: (0, 0, i)),
            pl.BlockSpec((length, bw), lambda i: (0, i)),
        ],
        out_specs=pl.BlockSpec((3, length, bw), lambda i: (0, 0, i)),
        out_shape=jax.ShapeDtypeStruct((3, length, columns), jnp.bfloat16),
        compiler_params=pltpu.CompilerParams(vmem_limit_bytes=32 << 20),
        cost_estimate=pl.CostEstimate(
            flops=60 * length * length * columns, bytes_accessed=14 * length * columns, transcendentals=0
        ),
        name="attend_back",
    )(count, qkv, cot)


def swapped(shard):
    peers = lax.axis_size("dp")
    half = peers // 2
    return lax.ppermute(shard, "dp", [(i, (i + half) % peers) for i in range(peers)])


def shards(projected, residue_counts, migrate_plan, out_weight, out_cotangent):
    sent = migrate_plan[0] > 0
    far_cot = swapped(out_cotangent[1])
    whole_weight = lax.all_gather(out_weight, "dp", axis=1, tiled=True)
    ctx = attend(projected, residue_counts)
    cot = jnp.where(sent, far_cot, out_cotangent[0])
    full_cot = lax.all_gather(cot, "tensor", axis=1, tiled=True)
    partial_value = dot(ctx, whole_weight, NN).astype(jnp.bfloat16)
    own = lax.psum_scatter(partial_value, "tensor", scatter_dimension=1, tiled=True)
    nothing = jnp.zeros_like(own)
    guest = swapped(jnp.where(sent, own, nothing))
    weight_term = dot(ctx, full_cot, TN).astype(jnp.bfloat16)
    grad_weight = lax.psum_scatter(weight_term, "dp", scatter_dimension=1, tiled=True)
    grad_context = dot(full_cot, whole_weight, NT).astype(jnp.bfloat16)
    grad_projected = attend_back(projected, residue_counts, grad_context)
    layer_out = jnp.stack([jnp.where(sent, nothing, own), guest])
    return (layer_out, grad_projected, grad_weight.astype(jnp.float32))


def solution(mesh):
    in_specs = (
        P(None, "dp", "tensor"),
        P("dp"),
        P("dp"),
        P("tensor", "dp"),
        P("dp", None, "tensor"),
    )
    out_specs = (P("dp", None, "tensor"), P(None, "dp", "tensor"), P("tensor", "dp"))
    return jax.shard_map(shards, mesh=mesh, in_specs=in_specs, out_specs=out_specs, check_vma=False)
```

```python
import functools

import jax
import jax.numpy as jnp
from jax import lax
from jax.experimental import pallas as pl
from jax.experimental.pallas import tpu as pltpu
from jax.sharding import PartitionSpec as P

HEAD_DIM = 64
SCALE = HEAD_DIM ** (-0.5)
LOG2E = 1.4426950408889634
NT = (((1,), (1,)), ((), ()))
NN = (((1,), (0,)), ((), ()))
TN = (((0,), (0,)), ((), ()))


def dot(a, b, dims):
    return lax.dot_general(a, b, dims, preferred_element_type=jnp.float32)


def probs_t(k, q, live_keys):
    s = dot(k, q, NT) * (SCALE * LOG2E)
    s = jnp.where(live_keys, s, -1000000000.0)
    e = jnp.exp2(s - jnp.max(s, axis=0, keepdims=True))
    return e * (1.0 / jnp.sum(e, axis=0, keepdims=True))


def fwd_kernel(count_ref, qkv_ref, ctx_ref):
    length, width = ctx_ref.shape
    live = lax.broadcasted_iota(jnp.int32, (length, 1), 0) < count_ref[0]
    parts = []
    for h in range(width // HEAD_DIM):
        cols = slice(h * HEAD_DIM, (h + 1) * HEAD_DIM)
        p = probs_t(qkv_ref[1, :, cols], qkv_ref[0, :, cols], live).astype(jnp.bfloat16)
        parts.append(dot(p, qkv_ref[2, :, cols], TN))
    ctx = jnp.concatenate(parts, axis=1)
    ctx_ref[...] = jnp.where(live, ctx, 0.0).astype(jnp.bfloat16)


def bwd_kernel(count_ref, qkv_ref, cot_ref, out_ref):
    length, width = cot_ref.shape
    live = lax.broadcasted_iota(jnp.int32, (length, 1), 0) < count_ref[0]
    grads = ([], [], [])
    for h in range(width // HEAD_DIM):
        cols = slice(h * HEAD_DIM, (h + 1) * HEAD_DIM)
        q, k, v = qkv_ref[0, :, cols], qkv_ref[1, :, cols], qkv_ref[2, :, cols]
        cot = jnp.where(live, cot_ref[:, cols], jnp.bfloat16(0))
        p = probs_t(k, q, live)
        dp = dot(v, cot, NT).astype(jnp.bfloat16).astype(jnp.float32)
        t = p * dp
        ds = (t - p * jnp.sum(t, axis=0, keepdims=True)).astype(jnp.bfloat16)
        grads[0].append(dot(ds, k, TN) * SCALE)
        grads[1].append(dot(ds, q, NN) * SCALE)
        grads[2].append(dot(p.astype(jnp.bfloat16), cot, NN))
    for i in range(3):
        out_ref[i] = jnp.concatenate(grads[i], axis=1).astype(jnp.bfloat16)


def block_width(columns):
    return 128 if columns % 128 == 0 else columns


def attend(qkv, count):
    _, length, columns = qkv.shape
    bw = block_width(columns)
    return pl.pallas_call(
        fwd_kernel,
        grid=(columns // bw,),
        in_specs=[
            pl.BlockSpec(memory_space=pltpu.SMEM),
            pl.BlockSpec((3, length, bw), lambda i: (0, 0, i)),
        ],
        out_specs=pl.BlockSpec((length, bw), lambda i: (0, i)),
        out_shape=jax.ShapeDtypeStruct((length, columns), jnp.bfloat16),
        compiler_params=pltpu.CompilerParams(vmem_limit_bytes=32 << 20),
        cost_estimate=pl.CostEstimate(
            flops=20 * length * length * columns, bytes_accessed=8 * length * columns, transcendentals=0
        ),
        name="attend",
    )(count, qkv)


def attend_back(qkv, count, cot):
    _, length, columns = qkv.shape
    bw = block_width(columns)
    return pl.pallas_call(
        bwd_kernel,
        grid=(columns // bw,),
        in_specs=[
            pl.BlockSpec(memory_space=pltpu.SMEM),
            pl.BlockSpec((3, length, bw), lambda i: (0, 0, i)),
            pl.BlockSpec((length, bw), lambda i: (0, i)),
        ],
        out_specs=pl.BlockSpec((3, length, bw), lambda i: (0, 0, i)),
        out_shape=jax.ShapeDtypeStruct((3, length, columns), jnp.bfloat16),
        compiler_params=pltpu.CompilerParams(vmem_limit_bytes=32 << 20),
        cost_estimate=pl.CostEstimate(
            flops=60 * length * length * columns, bytes_accessed=14 * length * columns, transcendentals=0
        ),
        name="attend_back",
    )(count, qkv, cot)


def swapped(shard):
    peers = lax.axis_size("dp")
    half = peers // 2
    return lax.ppermute(shard, "dp", [(i, (i + half) % peers) for i in range(peers)])


def shards(projected, residue_counts, migrate_plan, out_weight, out_cotangent):
    sent = migrate_plan[0] > 0
    far_cot = swapped(out_cotangent[1])
    whole_weight = lax.all_gather(out_weight, "dp", axis=1, tiled=True)
    ctx = attend(projected, residue_counts)
    far_cot, ctx = lax.optimization_barrier((far_cot, ctx))
    cot = jnp.where(sent, far_cot, out_cotangent[0])
    full_cot = lax.all_gather(cot, "tensor", axis=1, tiled=True)
    partial_value = dot(ctx, whole_weight, NN).astype(jnp.bfloat16)
    own = lax.psum_scatter(partial_value, "tensor", scatter_dimension=1, tiled=True)
    nothing = jnp.zeros_like(own)
    guest = swapped(jnp.where(sent, own, nothing))
    weight_term = dot(ctx, full_cot, TN).astype(jnp.bfloat16)
    grad_weight = lax.psum_scatter(weight_term, "dp", scatter_dimension=1, tiled=True)
    grad_context = dot(full_cot, whole_weight, NT).astype(jnp.bfloat16)
    grad_projected = attend_back(projected, residue_counts, grad_context)
    layer_out = jnp.stack([jnp.where(sent, nothing, own), guest])
    return (layer_out, grad_projected, grad_weight.astype(jnp.float32))


def solution(mesh):
    in_specs = (
        P(None, "dp", "tensor"),
        P("dp"),
        P("dp"),
        P("tensor", "dp"),
        P("dp", None, "tensor"),
    )
    out_specs = (P("dp", None, "tensor"), P(None, "dp", "tensor"), P("tensor", "dp"))
    return jax.shard_map(shards, mesh=mesh, in_specs=in_specs, out_specs=out_specs, check_vma=False)
```
